512 devices in a mesh: grid: 64 (over z, x), band: 8 (over y, core).
Axes of the slice: x: 4, y: 4, z: 16, core: 2. Of those that a mesh axis runs over, the one named last changes fastest.
Arguments:
- orbitals: float32 [8, 256, 128, 256], P('band', 'grid'), may hold values from -6 to 6
- potential: float32 [256, 128, 256], P('grid'), may hold values from -1 to 1
- partners: bfloat16 [8, 256, 128, 256], P('band', 'grid'), may hold values from -64 to 64
- owners: int32 [6], replicated, may hold values from 0 to 7, as said below
Outputs:
- filtered: float32 [8, 256, 128, 256], P('band', 'grid')
- intersection: float32 [6, 8], P(None, 'band')
The draws below stay inside these ranges and needn't reach their ends.
Inputs may be any that keep to these rules, and one draw needn't show every extreme that they name: `owners`: band indices; the same index may appear in several steps.
All inputs are finite; a program needn't handle non-finite values.
Results may differ from the reference program's by a relative error of at most 0.0025.
Values may be sent and summed in bfloat16 or wider, within the bound.
No kernel may reach another device: no remote copies, remote signals or barrier semaphores. Data moves between devices by JAX's collectives and lax.ppermute only.
A program may use at most 64 MiB of HBM per device.

```python
import math
import jax
import jax.numpy as jnp
from jax import lax

NX = 128
NY = 256
ORB_DEV = 1
STEPS = 6
NZ = 256
ORBS = 8


def draw_partners(key, part):
    key = jax.random.fold_in(key, 11)
    key_own, key_orb = jax.random.split(key, 2)
    plane = jnp.arange(NZ, dtype=jnp.float32) / NZ
    orbital_scale = jnp.exp(jax.random.uniform(key_orb, (ORBS,), jnp.float32, math.log(0.3), math.log(3.0)))
    base = jnp.clip(jax.random.normal(key_own, (ORBS, NZ, NX, NY), jnp.float32), -5.0, 5.0)
    plane_scale = jnp.power(10.0, plane) / 4.0
    values = base * plane_scale[None, :, None, None] * orbital_scale[:, None, None, None]
    return values.astype(jnp.bfloat16)


def draw_owners(key, part):
    key = jax.random.fold_in(key, 23)
    key_order, key_rest = jax.random.split(key, 2)
    highest = ORBS // ORB_DEV - 1
    flipped = jax.random.randint(key_order, (), 0, 2, jnp.int32)
    leading = jnp.stack([flipped * highest, (1 - flipped) * highest]).astype(jnp.int32)
    remaining = jax.random.randint(key_rest, (STEPS - 2,), 0, highest + 1, jnp.int32)
    return jnp.concatenate([leading, remaining], 0).astype(jnp.int32)


def level_of(own_key, dims, pieces, low, largest):
    level, own = 1.0, jax.random.fold_in(own_key, 6)
    for axis_at, parts in pieces:
        draws = jnp.exp(jax.random.uniform(jax.random.fold_in(own, axis_at), (parts,), jnp.float32, low / len(pieces), largest / len(pieces)))
        level = level * jnp.repeat(draws, dims[axis_at] // parts).reshape([-1 if axis == axis_at else 1 for axis in range(len(dims))])
    return level


def bell_draw(key, extent, deviation, most, cuts=(), kind=jnp.bfloat16):
    drawn = jax.random.normal(key, extent, jnp.float32) * deviation
    if len(cuts) > 0:
        drawn = level_of(key, extent, cuts, -0.22, 0.18) * drawn
    return jnp.clip(drawn, min=-most, max=most).astype(kind)


def setup_inputs(seed: int = 0) -> dict:
    keys = jax.random.split(jax.random.key(seed), 5)
    return {
        "orbitals": bell_draw(keys[0], (ORBS, NZ, NX, NY), 1.0, 6.0, ((0, 8), (1, 64)), jnp.float32),
        "potential": jnp.clip(jax.random.uniform(keys[1], (NZ, NX, NY), jnp.float32, -1.0, 1.0) * level_of(keys[1], (NZ, NX, NY), ((0, 64),), -0.4, 0.0), -1.0, 1.0),
        "partners": draw_partners(jax.random.fold_in(keys[4], 71), 0),
        "owners": draw_owners(jax.random.fold_in(keys[4], 71), 0),
    }


CENTER_SHIFT = 5.0
HALF_WIDTH = 4.0
NEAR_WEIGHT = 4.0 / 3.0
FAR_WEIGHT = -1.0 / 12.0


def hamiltonian(field, potential):
    laplace = -7.5 * field
    for spatial in (1, 2, 3):
        laplace = laplace + NEAR_WEIGHT * (jnp.roll(field, 1, spatial) + jnp.roll(field, -1, spatial))
        laplace = laplace + FAR_WEIGHT * (jnp.roll(field, 2, spatial) + jnp.roll(field, -2, spatial))
    return -0.5 * laplace + potential[None] * field


def reference(orbitals, potential, partners, owners):
    first = (hamiltonian(orbitals, potential) - CENTER_SHIFT * orbitals) / HALF_WIDTH
    filtered = 2.0 * (hamiltonian(first, potential) - CENTER_SHIFT * first) / HALF_WIDTH - orbitals
    rounded = filtered.astype(jnp.bfloat16)
    widened = partners.astype(jnp.float32)
    factor = float(NZ * NX * NY) ** -0.5
    gathered_rows = []
    for owner_step in range(STEPS):
        start = (owners[owner_step] * ORB_DEV).astype(jnp.int32)
        block = lax.dynamic_slice_in_dim(rounded, start, ORB_DEV, 0).astype(jnp.float32)
        gathered_rows.append(jnp.einsum("azxy,bzxy->ab", block, widened) * factor)
    return filtered, jnp.concatenate(gathered_rows, 0)
```

```python
import jax
import jax.numpy as jnp
from jax import lax
from jax.experimental import pallas as pl
from jax.experimental.pallas import tpu as pltpu
from jax.sharding import Mesh, PartitionSpec as P

STEPS = 6
ORBS = 8
CELLS = 256 * 128 * 256
FACTOR = float(CELLS) ** -0.5

DIAGONAL = 3.75 - 5.0
NEAR = -0.5 * (4.0 / 3.0) / 4.0
FAR = -0.5 * (-1.0 / 12.0) / 4.0

VMEM = pltpu.VMEM
SMEM = pltpu.SMEM
F32 = jnp.float32


def lateral(plane):
    rows, columns = plane.shape
    near = (
        pltpu.roll(plane, 1, 0)
        + pltpu.roll(plane, rows - 1, 0)
        + pltpu.roll(plane, 1, 1)
        + pltpu.roll(plane, columns - 1, 1)
    )
    far = (
        pltpu.roll(plane, 2, 0)
        + pltpu.roll(plane, rows - 2, 0)
        + pltpu.roll(plane, 2, 1)
        + pltpu.roll(plane, columns - 2, 1)
    )
    return near, far


def local_kernel(field_ref, potential_ref, low_ref, high_ref):
    planes = field_ref.shape[0]
    for z in range(planes):
        center = field_ref[z]
        near, far = lateral(center)
        for offset, weight in ((1, "near"), (2, "far")):
            for other in (z - offset, z + offset):
                if 0 <= other < planes:
                    if weight == "near":
                        near = near + field_ref[other]
                    else:
                        far = far + field_ref[other]
        part = (0.25 * (potential_ref[z] + DIAGONAL)) * center + (NEAR * near + FAR * far)
        half = low_ref if z < 2 else high_ref
        half[z % 2] = center
        half[2 + z % 2] = part


def filter_kernel(low_ref, high_ref, left_ref, right_ref, potential_ref, filtered_ref, rounded_ref, first_ref):
    f0, f1, f2, f3 = low_ref[0], low_ref[1], high_ref[0], high_ref[1]
    first_ref[0] = left_ref[2] + FAR * f0
    first_ref[1] = left_ref[3] + NEAR * f0 + FAR * f1
    first_ref[2] = low_ref[2] + NEAR * left_ref[1] + FAR * left_ref[0]
    first_ref[3] = low_ref[3] + FAR * left_ref[1]
    first_ref[4] = high_ref[2] + FAR * right_ref[0]
    first_ref[5] = high_ref[3] + NEAR * right_ref[0] + FAR * right_ref[1]
    first_ref[6] = right_ref[2] + NEAR * f3 + FAR * f2
    first_ref[7] = right_ref[3] + FAR * f3
    for z in range(4):
        center = first_ref[2 + z]
        near, far = lateral(center)
        near = near + (first_ref[1 + z] + first_ref[3 + z])
        far = far + (first_ref[z] + first_ref[4 + z])
        second = (0.25 * (potential_ref[z] + DIAGONAL)) * center + (NEAR * near + FAR * far)
        own = (low_ref if z < 2 else high_ref)[z % 2]
        filtered = 2.0 * second - own
        filtered_ref[z] = filtered
        rounded_ref[z] = filtered.astype(rounded_ref.dtype)


def products_kernel(rounded_ref, partners_ref, out_ref):
    for j in range(ORBS):
        partner = partners_ref[j].astype(F32)
        for o in range(ORBS):
            product = rounded_ref[o].astype(F32) * partner
            total = jnp.sum(product, axis=0, keepdims=True)
            row = total[:, :128] + total[:, 128:]
            for x in range(4):
                out_ref[x, j, pl.ds(o, 1), :] = row


def owners_kernel(owners_ref, parts_ref, out_ref):
    total = parts_ref[0]
    for k in range(1, parts_ref.shape[0]):
        total = total + parts_ref[k]
    row = lax.broadcasted_iota(jnp.int32, total.shape, 0)
    chosen = jnp.zeros_like(total)
    for s in range(STEPS):
        one = jnp.sum(jnp.where(row == owners_ref[s], total, 0.0), axis=0, keepdims=True)
        chosen = jnp.where(row == s, one, chosen)
    for k in range(out_ref.shape[0]):
        out_ref[k] = chosen


def last_kernel(parts_ref, out_ref):
    total = parts_ref[0]
    for k in range(1, parts_ref.shape[0]):
        total = total + parts_ref[k]
    out_ref[...] = jnp.sum(total, axis=1, keepdims=True)[:STEPS] * FACTOR


def call(kernel, shapes, args, spaces=None, scratch=()):
    spaces = spaces or [VMEM] * len(args)
    return pl.pallas_call(
        kernel,
        out_shape=shapes,
        in_specs=[pl.BlockSpec(memory_space=space) for space in spaces],
        out_specs=jax.tree.map(lambda _: pl.BlockSpec(memory_space=VMEM), shapes),
        scratch_shapes=list(scratch),
        compiler_params=pltpu.CompilerParams(vmem_limit_bytes=32 * 1024 * 1024),
    )(*args)


def shards(orbitals, potential, partners, owners):
    grid, band, layer = ("z", "x"), ("y", "core"), ("x", "y", "core")
    count = lax.axis_size(grid)
    up = [(i, (i + 1) % count) for i in range(count)]
    down = [(i, (i - 1) % count) for i in range(count)]
    _, planes, rows, columns = orbitals.shape
    shape = jax.ShapeDtypeStruct
    slab = shape((4, rows, columns), F32)

    low, high = call(local_kernel, (slab, slab), (orbitals[0], potential))
    left = lax.ppermute(high, grid, up)
    right = lax.ppermute(low, grid, down)
    pieces = (ORBS, planes * rows // ORBS, columns)
    partners = lax.all_to_all(partners.reshape(pieces), band, 0, 0, tiled=True)
    filtered, rounded = call(
        filter_kernel,
        (shape((planes, rows, columns), F32), shape((planes, rows, columns), jnp.bfloat16)),
        (low, high, left, right, potential),
        scratch=(pltpu.VMEM((8, rows, columns), F32),),
    )
    rounded = lax.all_to_all(rounded.reshape(pieces), band, 0, 0, tiled=True)
    parts = call(products_kernel, shape((4, ORBS, ORBS, 128), F32), (rounded, partners))
    parts = lax.all_to_all(parts.reshape(4 * ORBS, ORBS, 128), layer, 0, 0, tiled=True)
    depth = lax.axis_size("z")
    parts = call(owners_kernel, shape((depth, ORBS, 128), F32), (owners, parts), (SMEM, VMEM))
    parts = lax.all_to_all(parts, "z", 0, 0, tiled=True)
    intersection = call(last_kernel, shape((STEPS, 1), F32), (parts,))
    return filtered[None], intersection


def solution(mesh):
    fine = Mesh(mesh.devices.reshape(16, 4, 4, 2), ("z", "x", "y", "core"))
    grid, band = ("z", "x"), ("y", "core")
    in_specs = (P(band, grid, None, None), P(grid, None, None), P(band, grid, None, None), P())
    out_specs = (P(band, grid, None, None), P(None, band))
    return jax.shard_map(shards, mesh=fine, in_specs=in_specs, out_specs=out_specs, check_vma=False)
```

```python
import jax
import jax.numpy as jnp
from jax import lax
from jax.experimental import pallas as pl
from jax.experimental.pallas import tpu as pltpu
from jax.sharding import Mesh, PartitionSpec as P

STEPS = 6
ORBS = 8
CELLS = 256 * 128 * 256
FACTOR = float(CELLS) ** -0.5

DIAGONAL = 3.75 - 5.0
NEAR = -0.5 * (4.0 / 3.0) / 4.0
FAR = -0.5 * (-1.0 / 12.0) / 4.0

VMEM = pltpu.VMEM
SMEM = pltpu.SMEM
F32 = jnp.float32
BF16 = jnp.bfloat16


def lateral(plane):
    rows, columns = plane.shape
    near = (
        pltpu.roll(plane, 1, 0)
        + pltpu.roll(plane, rows - 1, 0)
        + pltpu.roll(plane, 1, 1)
        + pltpu.roll(plane, columns - 1, 1)
    )
    far = (
        pltpu.roll(plane, 2, 0)
        + pltpu.roll(plane, rows - 2, 0)
        + pltpu.roll(plane, 2, 1)
        + pltpu.roll(plane, columns - 2, 1)
    )
    return near, far


def split(value):
    high = value.astype(BF16)
    return high, (value - high.astype(F32)).astype(BF16)


def joined(ref, place):
    return ref[place].astype(F32) + ref[place + 1].astype(F32)


def edge(ref, near, far, near_part, far_part):
    ref[0], ref[1] = split(NEAR * near + FAR * far)
    ref[2] = near.astype(BF16)
    ref[3], ref[4] = split(NEAR * near_part + FAR * far_part)
    ref[5] = near_part.astype(BF16)


def local_kernel(field_ref, potential_ref, part_ref, low_ref, high_ref):
    planes = part_ref.shape[0]
    for z in range(planes):
        center = field_ref[z]
        near, far = lateral(center)
        for other in (z - 1, z + 1):
            if 0 <= other < planes:
                near = near + field_ref[other]
        for other in (z - 2, z + 2):
            if 0 <= other < planes:
                far = far + field_ref[other]
        part_ref[z] = (0.25 * (potential_ref[z] + DIAGONAL)) * center + (NEAR * near + FAR * far)
    edge(low_ref, field_ref[0], field_ref[1], part_ref[0], part_ref[1])
    edge(high_ref, field_ref[3], field_ref[2], part_ref[3], part_ref[2])


def find_places(owners_ref, places_ref):
    core = lax.axis_index("core")
    row = lax.broadcasted_iota(jnp.int32, places_ref.shape, 0)
    half = lax.broadcasted_iota(jnp.int32, places_ref.shape, 1) // 64
    places = jnp.full(places_ref.shape, 4, jnp.int32)
    for s in range(STEPS):
        owner = owners_ref[s]
        other = jnp.where(owner % 2 == core, 0, 1)
        places = jnp.where((row == s) & (half == other), owner // 2, places)
    places_ref[...] = places


def filter_kernel(
    owners_ref, field_ref, potential_ref, part_ref, left_ref, right_ref, filtered_ref, rounded_ref, places_ref, first_ref
):
    find_places(owners_ref, places_ref)
    first_ref[0] = part_ref[0] + joined(left_ref, 0)
    first_ref[1] = part_ref[1] + FAR * left_ref[2].astype(F32)
    first_ref[2] = part_ref[2] + FAR * right_ref[2].astype(F32)
    first_ref[3] = part_ref[3] + joined(right_ref, 0)
    f0, f1, f2, f3 = (field_ref[z] for z in range(4))
    outside = (
        joined(left_ref, 3) + ((NEAR * NEAR + FAR * FAR) * f0 + (NEAR * FAR) * f1),
        FAR * (left_ref[5].astype(F32) + (NEAR * f0 + FAR * f1)),
        FAR * (right_ref[5].astype(F32) + (NEAR * f3 + FAR * f2)),
        joined(right_ref, 3) + ((NEAR * NEAR + FAR * FAR) * f3 + (NEAR * FAR) * f2),
    )
    for z in range(4):
        center = first_ref[z]
        near, far = lateral(center)
        for other in (z - 1, z + 1):
            if 0 <= other < 4:
                near = near + first_ref[other]
        for other in (z - 2, z + 2):
            if 0 <= other < 4:
                far = far + first_ref[other]
        second = (0.25 * (potential_ref[z] + DIAGONAL)) * center + (NEAR * near + FAR * far) + outside[z]
        filtered = 2.0 * second - field_ref[z]
        filtered_ref[z] = filtered
        rounded_ref[z] = filtered.astype(BF16)


def products_kernel(own_ref, other_ref, partners_ref, out_ref):
    lane = lax.broadcasted_iota(jnp.int32, (1, 128), 1)
    for place in range(4):
        rows = []
        for rounded_ref in (own_ref, other_ref):
            total = jnp.zeros((8, 128), F32)
            for z in range(own_ref.shape[0]):
                product = rounded_ref[z].astype(F32) * partners_ref[place, z].astype(F32)
                folded = jnp.sum(product.reshape(-1, 8, product.shape[-1]), axis=0)
                total = total + (folded[:, :128] + folded[:, 128:])
            row = jnp.sum(total, axis=0, keepdims=True)
            rows.append(row + pltpu.roll(row, 64, 1))
        both = jnp.where(lane < 64, rows[0], rows[1])
        for x in range(4):
            out_ref[pl.ds(4 * x + place, 1), :] = both


def owners_kernel(places_ref, parts_ref, out_ref):
    total = parts_ref[0:4]
    for x in range(1, 4):
        total = total + parts_ref[4 * x : 4 * x + 4]
    places = places_ref[...]
    chosen = jnp.zeros(places.shape, F32)
    for y in range(4):
        chosen = jnp.where(places == y, total[(y + 2) % 4 : (y + 2) % 4 + 1], chosen)
    sums = jnp.sum(chosen, axis=1, keepdims=True)
    row = lax.broadcasted_iota(jnp.int32, chosen.shape, 0)
    lane = lax.broadcasted_iota(jnp.int32, chosen.shape, 1)
    line = jnp.sum(jnp.where(row == lane, sums, 0.0), axis=0, keepdims=True)
    out_ref[...] = jnp.broadcast_to(line, out_ref.shape)


def last_kernel(parts_ref, out_ref):
    out_ref[...] = jnp.sum(parts_ref[...], axis=0, keepdims=True)[:, :STEPS] * FACTOR


def call(kernel, shapes, args, spaces=None, scratch=(), cost=None):
    spaces = spaces or [VMEM] * len(args)
    return pl.pallas_call(
        kernel,
        out_shape=shapes,
        in_specs=[pl.BlockSpec(memory_space=space) for space in spaces],
        out_specs=jax.tree.map(lambda _: pl.BlockSpec(memory_space=VMEM), shapes),
        scratch_shapes=list(scratch),
        compiler_params=pltpu.CompilerParams(vmem_limit_bytes=8 * 1024 * 1024),
        cost_estimate=cost,
    )(*args)


def from_middle(size, first):
    return [[(first + i) % size for i in range(size)]]


def shards(orbitals, potential, partners, owners):
    grid = ("z", "x")
    count = lax.axis_size(grid)
    up = [(i, (i + 1) % count) for i in range(count)]
    down = [(i, (i - 1) % count) for i in range(count)]
    _, planes, rows, columns = orbitals.shape
    shape = jax.ShapeDtypeStruct
    slab, edges = shape((planes, rows, columns), F32), shape((6, rows, columns), BF16)

    copies = jnp.broadcast_to(partners, (4,) + partners.shape[1:])
    copies, orbitals = lax.optimization_barrier((copies, orbitals))
    part, low, high = call(local_kernel, (slab, edges, edges), (orbitals[0], potential))
    left = lax.ppermute(high, grid, up)
    right = lax.ppermute(low, grid, down)
    partners = lax.all_to_all(copies, "y", 0, 0, tiled=True, axis_index_groups=from_middle(4, 2))
    filtered, rounded, places = call(
        filter_kernel,
        (slab, shape(slab.shape, BF16), shape((ORBS, 128), jnp.int32)),
        (owners, orbitals[0], potential, part, left, right),
        (SMEM,) + (VMEM,) * 5,
        (pltpu.VMEM(slab.shape, F32),),
        cost=pl.CostEstimate(flops=10**11, bytes_accessed=10**6, transcendentals=0),
    )
    other = lax.ppermute(rounded, "core", [(0, 1), (1, 0)])
    parts = call(products_kernel, shape((16, 128), F32), (rounded, other, partners))
    parts = lax.all_to_all(parts, ("x", "y"), 0, 0, tiled=True, axis_index_groups=from_middle(16, 10))
    parts = call(owners_kernel, shape((lax.axis_size("z"), 128), F32), (places, parts))
    parts = lax.all_to_all(parts, "z", 0, 0, tiled=True, axis_index_groups=from_middle(16, 8))
    intersection = call(last_kernel, shape((1, STEPS), F32), (parts,))
    return filtered[None], intersection.T


def solution(mesh):
    fine = Mesh(mesh.devices.reshape(16, 4, 4, 2), ("z", "x", "y", "core"))
    grid, band = ("z", "x"), ("y", "core")
    in_specs = (P(band, grid, None, None), P(grid, None, None), P(band, grid, None, None), P())
    out_specs = (P(band, grid, None, None), P(None, band))
    return jax.shard_map(shards, mesh=fine, in_specs=in_specs, out_specs=out_specs, check_vma=False)
```

```python
import jax
import jax.numpy as jnp
from jax import lax
from jax.experimental import pallas as pl
from jax.experimental.pallas import tpu as pltpu
from jax.sharding import Mesh, PartitionSpec as P

STEPS = 6
ORBS = 8
CELLS = 256 * 128 * 256
FACTOR = float(CELLS) ** -0.5

DIAGONAL = 3.75 - 5.0
NEAR = -0.5 * (4.0 / 3.0) / 4.0
FAR = -0.5 * (-1.0 / 12.0) / 4.0

VMEM = pltpu.VMEM
SMEM = pltpu.SMEM
F32 = jnp.float32
BF16 = jnp.bfloat16

Z_FIRST = 8
LAYER_FIRST = 21
Y_FIRST = 2


def lateral(plane):
    rows, columns = plane.shape
    near = (
        pltpu.roll(plane, 1, 0)
        + pltpu.roll(plane, rows - 1, 0)
        + pltpu.roll(plane, 1, 1)
        + pltpu.roll(plane, columns - 1, 1)
    )
    far = (
        pltpu.roll(plane, 2, 0)
        + pltpu.roll(plane, rows - 2, 0)
        + pltpu.roll(plane, 2, 1)
        + pltpu.roll(plane, columns - 2, 1)
    )
    return near, far


def store_edge(ref, planes):
    rows = planes[0].shape[0]
    place = lax.broadcasted_iota(jnp.int32, (16, planes[0].shape[1]), 0)
    exponents = jnp.zeros(place.shape, jnp.int32)
    for k, plane in enumerate(planes):
        largest = jnp.maximum(jnp.max(jnp.abs(plane), axis=0, keepdims=True), 1e-30)
        exponent = jnp.floor(jnp.log2(largest)) + 2.0
        ref[pl.ds(k * rows, rows), :] = jnp.round(plane * jnp.exp2(15.0 - exponent)).astype(jnp.int32).astype(jnp.int16)
        exponents = jnp.where(place == k, exponent.astype(jnp.int32), exponents)
    ref[pl.ds(len(planes) * rows, 16), :] = exponents.astype(jnp.int16)


def load_edge(ref, k, rows=128):
    exponent = ref[pl.ds(4 * rows, 16), :].astype(jnp.int32).astype(F32)[k : k + 1]
    return ref[pl.ds(k * rows, rows), :].astype(jnp.int32).astype(F32) * jnp.exp2(exponent - 15.0)


def edge(ref, near, far, near_part, far_part):
    store_edge(ref, (NEAR * near + FAR * far, near, NEAR * near_part + FAR * far_part, near_part))


def local_kernel(field_ref, potential_ref, part_ref, low_ref, high_ref):
    planes = part_ref.shape[0]
    for z in range(planes):
        center = field_ref[z]
        near, far = lateral(center)
        for other in (z - 1, z + 1):
            if 0 <= other < planes:
                near = near + field_ref[other]
        for other in (z - 2, z + 2):
            if 0 <= other < planes:
                far = far + field_ref[other]
        part_ref[z] = (0.25 * (potential_ref[z] + DIAGONAL)) * center + (NEAR * near + FAR * far)
    edge(low_ref, field_ref[0], field_ref[1], part_ref[0], part_ref[1])
    edge(high_ref, field_ref[3], field_ref[2], part_ref[3], part_ref[2])


def member(place, size, first):
    return (first + place) % size


def product_rows(rounded_ref, partners_ref, out_ref):
    for k in range(partners_ref.shape[0]):
        total = jnp.zeros((8, 128), F32)
        for z in range(partners_ref.shape[1]):
            product = rounded_ref[z].astype(F32) * partners_ref[k, z].astype(F32)
            folded = jnp.sum(product.reshape(-1, 8, product.shape[-1]), axis=0)
            total = total + (folded[:, :128] + folded[:, 128:])
        out_ref[pl.ds(k, 1), :] = jnp.sum(total, axis=0, keepdims=True)


def filter_kernel(
    owners_ref, field_ref, potential_ref, part_ref, left_ref, right_ref, partners_ref, filtered_ref, rounded_ref, rows_ref, places_ref, first_ref
):
    row = lax.broadcasted_iota(jnp.int32, places_ref.shape, 0)
    places = jnp.full(places_ref.shape, ORBS, jnp.int32)
    for s in range(STEPS):
        places = jnp.where(row == s, owners_ref[s], places)
    places_ref[...] = places
    first_ref[0] = part_ref[0] + load_edge(left_ref, 0)
    first_ref[1] = part_ref[1] + FAR * load_edge(left_ref, 1)
    first_ref[2] = part_ref[2] + FAR * load_edge(right_ref, 1)
    first_ref[3] = part_ref[3] + load_edge(right_ref, 0)
    f0, f1, f2, f3 = (field_ref[z] for z in range(4))
    outside = (
        load_edge(left_ref, 2) + ((NEAR * NEAR + FAR * FAR) * f0 + (NEAR * FAR) * f1),
        FAR * (load_edge(left_ref, 3) + (NEAR * f0 + FAR * f1)),
        FAR * (load_edge(right_ref, 3) + (NEAR * f3 + FAR * f2)),
        load_edge(right_ref, 2) + ((NEAR * NEAR + FAR * FAR) * f3 + (NEAR * FAR) * f2),
    )
    for z in range(4):
        center = first_ref[z]
        near, far = lateral(center)
        for other in (z - 1, z + 1):
            if 0 <= other < 4:
                near = near + first_ref[other]
        for other in (z - 2, z + 2):
            if 0 <= other < 4:
                far = far + first_ref[other]
        second = (0.25 * (potential_ref[z] + DIAGONAL)) * center + (NEAR * near + FAR * far) + outside[z]
        filtered = 2.0 * second - field_ref[z]
        filtered_ref[z] = filtered
        rounded_ref[z] = filtered.astype(BF16)
    product_rows(rounded_ref, partners_ref, rows_ref)


def products_kernel(rounded_ref, partners_ref, own_ref, out_ref, other_ref):
    product_rows(rounded_ref, partners_ref, other_ref)
    core = lax.axis_index("core")
    own, other = own_ref[...], other_ref[...]
    rows = jnp.where(core == 0, own, other), jnp.where(core == 0, other, own)
    for place in range(out_ref.shape[0]):
        device = member(place, out_ref.shape[0], LAYER_FIRST)
        y = (device // 2 - Y_FIRST) % 4
        out_ref[pl.ds(place, 1), :] = rows[device % 2][y : y + 1]


def owners_kernel(places_ref, parts_ref, out_ref):
    totals = [jnp.zeros((1, 128), F32)] * ORBS
    for place in range(parts_ref.shape[0]):
        owner = member(place, parts_ref.shape[0], LAYER_FIRST) % ORBS
        totals[owner] = totals[owner] + parts_ref[pl.ds(place, 1), :]
    places = places_ref[...]
    chosen = jnp.zeros(places.shape, F32)
    for owner in range(ORBS):
        chosen = jnp.where(places == owner, totals[owner], chosen)
    sums = jnp.sum(chosen, axis=1, keepdims=True)
    row = lax.broadcasted_iota(jnp.int32, chosen.shape, 0)
    lane = lax.broadcasted_iota(jnp.int32, chosen.shape, 1)
    line = jnp.sum(jnp.where(row == lane, sums, 0.0), axis=0, keepdims=True)
    out_ref[...] = jnp.broadcast_to(line, out_ref.shape)


def last_kernel(parts_ref, out_ref):
    out_ref[...] = jnp.sum(parts_ref[...], axis=0, keepdims=True)[:, :STEPS] * FACTOR


def call(kernel, shapes, args, spaces=None, scratch=(), cost=None):
    spaces = spaces or [VMEM] * len(args)
    return pl.pallas_call(
        kernel,
        out_shape=shapes,
        in_specs=[pl.BlockSpec(memory_space=space) for space in spaces],
        out_specs=jax.tree.map(lambda _: pl.BlockSpec(memory_space=VMEM), shapes),
        scratch_shapes=list(scratch),
        compiler_params=pltpu.CompilerParams(vmem_limit_bytes=8 * 1024 * 1024),
        cost_estimate=cost,
    )(*args)


def from_middle(size, first):
    return [[(first + i) % size for i in range(size)]]


def shards(orbitals, potential, partners, owners):
    grid = ("z", "x")
    count = lax.axis_size(grid)
    up = [(i, (i + 1) % count) for i in range(count)]
    down = [(i, (i - 1) % count) for i in range(count)]
    _, planes, rows, columns = orbitals.shape
    shape = jax.ShapeDtypeStruct
    slab, edges = shape((planes, rows, columns), F32), shape((4 * rows + 16, columns), jnp.int16)

    copies = jnp.broadcast_to(partners, (4,) + partners.shape[1:])
    copies, orbitals = lax.optimization_barrier((copies, orbitals))
    partners = lax.all_to_all(copies, "y", 0, 0, tiled=True, axis_index_groups=from_middle(4, Y_FIRST))
    part, low, high = call(local_kernel, (slab, edges, edges), (orbitals[0], potential))
    left = lax.ppermute(high, grid, up)
    right = lax.ppermute(low, grid, down)
    partners, left = lax.optimization_barrier((partners, left))
    others = lax.ppermute(partners, "core", [(0, 1), (1, 0)])
    filtered, rounded, own, places = call(
        filter_kernel,
        (slab, shape(slab.shape, BF16), shape((4, 128), F32), shape((ORBS, 128), jnp.int32)),
        (owners, orbitals[0], potential, part, left, right, partners),
        (SMEM,) + (VMEM,) * 6,
        (pltpu.VMEM(slab.shape, F32),),
        cost=pl.CostEstimate(flops=10**10, bytes_accessed=10**6, transcendentals=0),
    )
    parts = call(products_kernel, shape((4 * ORBS, 128), F32), (rounded, others, own), scratch=(pltpu.VMEM((4, 128), F32),))
    layer = ("x", "y", "core")
    parts = lax.all_to_all(parts, layer, 0, 0, tiled=True, axis_index_groups=from_middle(4 * ORBS, LAYER_FIRST))
    depth = lax.axis_size("z")
    parts = call(owners_kernel, shape((depth, 128), F32), (places, parts))
    parts = lax.all_to_all(parts, "z", 0, 0, tiled=True, axis_index_groups=from_middle(depth, Z_FIRST))
    intersection = call(last_kernel, shape((1, STEPS), F32), (parts,))
    return filtered[None], intersection.T


def solution(mesh):
    fine = Mesh(mesh.devices.reshape(16, 4, 4, 2), ("z", "x", "y", "core"))
    grid, band = ("z", "x"), ("y", "core")
    in_specs = (P(band, grid, None, None), P(grid, None, None), P(band, grid, None, None), P())
    out_specs = (P(band, grid, None, None), P(None, band))
    return jax.shard_map(shards, mesh=fine, in_specs=in_specs, out_specs=out_specs, check_vma=False)
```

```python
import jax
import jax.numpy as jnp
from jax import lax
from jax.experimental import pallas as pl
from jax.experimental.pallas import tpu as pltpu
from jax.sharding import Mesh, PartitionSpec as P

STEPS = 6
ORBS = 8
CELLS = 256 * 128 * 256
FACTOR = float(CELLS) ** -0.5

DIAGONAL = 3.75 - 5.0
NEAR = -0.5 * (4.0 / 3.0) / 4.0
FAR = -0.5 * (-1.0 / 12.0) / 4.0

VMEM = pltpu.VMEM
SMEM = pltpu.SMEM
F32 = jnp.float32
BF16 = jnp.bfloat16

ROWS = 32

Z_FIRST = 8
LAYER_FIRST = 21
Y_FIRST = 0


def lateral(ref, z, start, count):
    rows, columns = ref.shape[1:]
    if start == 0:
        wide = jnp.concatenate([ref[z, rows - 8 : rows], ref[z, 0 : count + 8]], axis=0)
    elif start + count == rows:
        wide = jnp.concatenate([ref[z, start - 8 : rows], ref[z, 0:8]], axis=0)
    else:
        wide = ref[z, start - 8 : start + count + 8]
    center = wide[8 : 8 + count]
    near = pltpu.roll(center, 1, 1) + pltpu.roll(center, columns - 1, 1)
    far = pltpu.roll(center, 2, 1) + pltpu.roll(center, columns - 2, 1)
    near = near + (pltpu.roll(wide, 1, 0)[8 : 8 + count] + pltpu.roll(wide, count + 15, 0)[8 : 8 + count])
    far = far + (pltpu.roll(wide, 2, 0)[8 : 8 + count] + pltpu.roll(wide, count + 14, 0)[8 : 8 + count])
    return center, near, far


def stencil(ref, potential_ref, z, start, count):
    block = pl.ds(start, count)
    center, near, far = lateral(ref, z, start, count)
    for other in (z - 1, z + 1):
        if 0 <= other < ref.shape[0]:
            near = near + ref[other, block]
    for other in (z - 2, z + 2):
        if 0 <= other < ref.shape[0]:
            far = far + ref[other, block]
    return (0.25 * (potential_ref[z, block] + DIAGONAL)) * center + (NEAR * near + FAR * far)


def store_edge(ref, planes):
    rows = planes[0].shape[0]
    place = lax.broadcasted_iota(jnp.int32, (16, planes[0].shape[1]), 0)
    exponents = jnp.zeros(place.shape, jnp.int32)
    for k, plane in enumerate(planes):
        largest = jnp.maximum(jnp.max(jnp.abs(plane), axis=0, keepdims=True), 1e-30)
        exponent = jnp.floor(jnp.log2(largest)) + 2.0
        ref[pl.ds(k * rows, rows), :] = jnp.round(plane * jnp.exp2(15.0 - exponent)).astype(jnp.int32).astype(jnp.int16)
        exponents = jnp.where(place == k, exponent.astype(jnp.int32), exponents)
    ref[pl.ds(len(planes) * rows, 16), :] = exponents.astype(jnp.int16)


def load_scales(ref):
    exponents = ref[pl.ds(ref.shape[0] - 16, 16), :].astype(jnp.int32).astype(F32)
    return jnp.exp2(exponents - 15.0)


def load_edge(ref, scales, k, start, count):
    rows = (ref.shape[0] - 16) // 4
    return ref[pl.ds(k * rows + start, count), :].astype(jnp.int32).astype(F32) * scales[k : k + 1]


def edge(ref, near, far, near_part, far_part):
    store_edge(ref, (NEAR * near + FAR * far, near, NEAR * near_part + FAR * far_part, near_part))


def local_kernel(field_ref, potential_ref, part_ref, low_ref, high_ref):
    planes, rows, _ = part_ref.shape
    for z in range(planes):
        for start in range(0, rows, ROWS):
            part_ref[z, pl.ds(start, ROWS)] = stencil(field_ref, potential_ref, z, start, ROWS)
    edge(low_ref, field_ref[0], field_ref[1], part_ref[0], part_ref[1])
    edge(high_ref, field_ref[3], field_ref[2], part_ref[3], part_ref[2])


def member(place, size, first):
    return (first + place) % size


def fold(product):
    folded = jnp.sum(product.reshape(-1, 8, product.shape[-1]), axis=0)
    return folded[:, :128] + folded[:, 128:]


def product_rows(rounded_ref, partners_ref, out_ref):
    count, planes, rows, _ = partners_ref.shape
    totals = [jnp.zeros((8, 128), F32)] * count
    for z in range(planes):
        for start in range(0, rows, ROWS):
            rounded = rounded_ref[z, pl.ds(start, ROWS)].astype(F32)
            for k in range(count):
                totals[k] = totals[k] + fold(rounded * partners_ref[k, z, pl.ds(start, ROWS)].astype(F32))
    for k, total in enumerate(totals):
        out_ref[pl.ds(k, 1), :] = jnp.sum(total, axis=0, keepdims=True)


def filter_kernel(
    field_ref, potential_ref, part_ref, left_ref, right_ref, partners_ref, filtered_hbm, rounded_ref, rows_ref, first_ref, filtered_ref, sems
):
    planes, rows, _ = part_ref.shape
    sides = (left_ref, load_scales(left_ref), 0, 1), (right_ref, load_scales(right_ref), 3, 2)
    for ref, scales, near, far in sides:
        for start in range(0, rows, ROWS):
            block = pl.ds(start, ROWS)
            first_ref[near, block] = part_ref[near, block] + load_edge(ref, scales, 0, start, ROWS)
            first_ref[far, block] = part_ref[far, block] + FAR * load_edge(ref, scales, 1, start, ROWS)
    totals = [jnp.zeros((8, 128), F32)] * partners_ref.shape[0]
    copies = []
    for ref, scales, nearest, second in sides:
        for z in (nearest, second):
            for start in range(0, rows, ROWS):
                block = pl.ds(start, ROWS)
                value = stencil(first_ref, potential_ref, z, start, ROWS)
                f0, f1 = field_ref[nearest, block], field_ref[second, block]
                if z == nearest:
                    value = value + (load_edge(ref, scales, 2, start, ROWS) + ((NEAR * NEAR + FAR * FAR) * f0 + (NEAR * FAR) * f1))
                else:
                    value = value + FAR * (load_edge(ref, scales, 3, start, ROWS) + (NEAR * f0 + FAR * f1))
                filtered = 2.0 * value - (f0 if z == nearest else f1)
                filtered_ref[z, block] = filtered
                rounded = filtered.astype(BF16)
                rounded_ref[z, block] = rounded
                rounded = rounded.astype(F32)
                for k in range(len(totals)):
                    totals[k] = totals[k] + fold(rounded * partners_ref[k, z, block].astype(F32))
            copy = pltpu.make_async_copy(filtered_ref.at[z], filtered_hbm.at[z], sems.at[z])
            copy.start()
            copies.append(copy)
    for k, total in enumerate(totals):
        rows_ref[pl.ds(k, 1), :] = jnp.sum(total, axis=0, keepdims=True)
    for copy in copies:
        copy.wait()


def products_kernel(rounded_ref, partners_ref, own_ref, out_ref, other_ref):
    product_rows(rounded_ref, partners_ref, other_ref)
    core = lax.axis_index("core")
    own, other = own_ref[...], other_ref[...]
    rows = jnp.where(core == 0, own, other), jnp.where(core == 0, other, own)
    for place in range(out_ref.shape[0]):
        device = member(place, out_ref.shape[0], LAYER_FIRST)
        y = (device // 2 - Y_FIRST) % 4
        out_ref[pl.ds(place, 1), :] = rows[device % 2][y : y + 1]


def owners_kernel(places_ref, parts_ref, out_ref):
    totals = [jnp.zeros((1, 128), F32)] * ORBS
    for place in range(parts_ref.shape[0]):
        owner = member(place, parts_ref.shape[0], LAYER_FIRST) % ORBS
        totals[owner] = totals[owner] + parts_ref[pl.ds(place, 1), :]
    places = places_ref[...]
    chosen = jnp.zeros(places.shape, F32)
    for owner in range(ORBS):
        chosen = jnp.where(places == owner, totals[owner], chosen)
    sums = jnp.sum(chosen, axis=1, keepdims=True)
    row = lax.broadcasted_iota(jnp.int32, chosen.shape, 0)
    lane = lax.broadcasted_iota(jnp.int32, chosen.shape, 1)
    line = jnp.sum(jnp.where(row == lane, sums, 0.0), axis=0, keepdims=True)
    out_ref[...] = jnp.broadcast_to(line, out_ref.shape)


def last_kernel(parts_ref, out_ref):
    out_ref[...] = jnp.sum(parts_ref[...], axis=0, keepdims=True)[:, :STEPS] * FACTOR


def call(kernel, shapes, args, spaces=None, scratch=(), cost=None, out_spaces=None):
    spaces = spaces or [VMEM] * len(args)
    return pl.pallas_call(
        kernel,
        out_shape=shapes,
        in_specs=[pl.BlockSpec(memory_space=space) for space in spaces],
        out_specs=[pl.BlockSpec(memory_space=space) for space in out_spaces or [VMEM] * len(shapes)],
        scratch_shapes=list(scratch),
        compiler_params=pltpu.CompilerParams(vmem_limit_bytes=8 * 1024 * 1024),
        cost_estimate=cost,
    )(*args)


def from_middle(size, first):
    return [[(first + i) % size for i in range(size)]]


def shards(orbitals, potential, partners, owners):
    grid = ("z", "x")
    count = lax.axis_size(grid)
    up = [(i, (i + 1) % count) for i in range(count)]
    down = [(i, (i - 1) % count) for i in range(count)]
    _, planes, rows, columns = orbitals.shape
    shape = jax.ShapeDtypeStruct
    slab, edges = shape((planes, rows, columns), F32), shape((4 * rows + 16, columns), jnp.int16)

    copies = jnp.broadcast_to(partners, (4,) + partners.shape[1:])
    copies, orbitals = lax.optimization_barrier((copies, orbitals))
    partners = lax.all_to_all(copies, "y", 0, 0, tiled=True, axis_index_groups=from_middle(4, Y_FIRST))
    part, low, high = call(local_kernel, (slab, edges, edges), (orbitals[0], potential))
    left = lax.ppermute(high, grid, up)
    right = lax.ppermute(low, grid, down)
    owners, left = lax.optimization_barrier((owners, left))
    places = jnp.broadcast_to(jnp.pad(owners, (0, ORBS - STEPS), constant_values=ORBS)[:, None], (ORBS, 128))
    partners, places = lax.optimization_barrier((partners, places))
    others = lax.ppermute(partners, "core", [(0, 1), (1, 0)])
    filtered, rounded, own = call(
        filter_kernel,
        (slab, shape(slab.shape, BF16), shape((4, 128), F32)),
        (orbitals[0], potential, part, left, right, partners),
        scratch=(pltpu.VMEM(slab.shape, F32), pltpu.VMEM(slab.shape, F32), pltpu.SemaphoreType.DMA((planes,))),
        cost=pl.CostEstimate(flops=10**10, bytes_accessed=10**6, transcendentals=0),
        out_spaces=(pl.ANY, VMEM, VMEM),
    )
    parts = call(products_kernel, (shape((4 * ORBS, 128), F32),), (rounded, others, own), scratch=(pltpu.VMEM((4, 128), F32),))[0]
    layer = ("x", "y", "core")
    parts = lax.all_to_all(parts, layer, 0, 0, tiled=True, axis_index_groups=from_middle(4 * ORBS, LAYER_FIRST))
    depth = lax.axis_size("z")
    parts = call(owners_kernel, (shape((depth, 128), F32),), (places, parts))[0]
    parts = lax.all_to_all(parts, "z", 0, 0, tiled=True, axis_index_groups=from_middle(depth, Z_FIRST))
    intersection = call(last_kernel, (shape((1, STEPS), F32),), (parts,))[0]
    return filtered[None], intersection.T


def solution(mesh):
    fine = Mesh(mesh.devices.reshape(16, 4, 4, 2), ("z", "x", "y", "core"))
    grid, band = ("z", "x"), ("y", "core")
    in_specs = (P(band, grid, None, None), P(grid, None, None), P(band, grid, None, None), P())
    out_specs = (P(band, grid, None, None), P(None, band))
    return jax.shard_map(shards, mesh=fine, in_specs=in_specs, out_specs=out_specs, check_vma=False)
```

```python
import jax
import jax.numpy as jnp
from jax import lax
from jax.experimental import pallas as pl
from jax.experimental.pallas import tpu as pltpu
from jax.sharding import Mesh, PartitionSpec as P

STEPS = 6
ORBS = 8
CELLS = 256 * 128 * 256
FACTOR = float(CELLS) ** -0.5

DIAGONAL = 3.75 - 5.0
NEAR = -0.5 * (4.0 / 3.0) / 4.0
FAR = -0.5 * (-1.0 / 12.0) / 4.0

VMEM = pltpu.VMEM
SMEM = pltpu.SMEM
F32 = jnp.float32
BF16 = jnp.bfloat16

ROWS = 32

Z_FIRST = 8
LAYER_FIRST = 21
Y_FIRST = 0


def lateral(ref, z, start, count):
    rows, columns = ref.shape[1:]
    if start == 0:
        wide = jnp.concatenate([ref[z, rows - 8 : rows], ref[z, 0 : count + 8]], axis=0)
    elif start + count == rows:
        wide = jnp.concatenate([ref[z, start - 8 : rows], ref[z, 0:8]], axis=0)
    else:
        wide = ref[z, start - 8 : start + count + 8]
    center = wide[8 : 8 + count]
    near = pltpu.roll(center, 1, 1) + pltpu.roll(center, columns - 1, 1)
    far = pltpu.roll(center, 2, 1) + pltpu.roll(center, columns - 2, 1)
    near = near + (pltpu.roll(wide, 1, 0)[8 : 8 + count] + pltpu.roll(wide, count + 15, 0)[8 : 8 + count])
    far = far + (pltpu.roll(wide, 2, 0)[8 : 8 + count] + pltpu.roll(wide, count + 14, 0)[8 : 8 + count])
    return center, near, far


def stencil(ref, potential_ref, z, start, count):
    block = pl.ds(start, count)
    center, near, far = lateral(ref, z, start, count)
    for other in (z - 1, z + 1):
        if 0 <= other < ref.shape[0]:
            near = near + ref[other, block]
    for other in (z - 2, z + 2):
        if 0 <= other < ref.shape[0]:
            far = far + ref[other, block]
    return (0.25 * (potential_ref[z, block] + DIAGONAL)) * center + (NEAR * near + FAR * far)


def store_edge(ref, planes):
    rows = planes[0].shape[0]
    place = lax.broadcasted_iota(jnp.int32, (16, planes[0].shape[1]), 0)
    exponents = jnp.zeros(place.shape, jnp.int32)
    for k, plane in enumerate(planes):
        largest = jnp.maximum(jnp.max(jnp.abs(plane), axis=0, keepdims=True), 1e-30)
        exponent = jnp.floor(jnp.log2(largest)) + 2.0
        ref[pl.ds(k * rows, rows), :] = jnp.round(plane * jnp.exp2(15.0 - exponent)).astype(jnp.int32).astype(jnp.int16)
        exponents = jnp.where(place == k, exponent.astype(jnp.int32), exponents)
    ref[pl.ds(len(planes) * rows, 16), :] = exponents.astype(jnp.int16)


def load_scales(ref):
    exponents = ref[pl.ds(ref.shape[0] - 16, 16), :].astype(jnp.int32).astype(F32)
    return jnp.exp2(exponents - 15.0)


def load_edge(ref, scales, k, start, count):
    rows = (ref.shape[0] - 16) // 4
    return ref[pl.ds(k * rows + start, count), :].astype(jnp.int32).astype(F32) * scales[k : k + 1]


def edge(ref, near, far, near_part, far_part):
    store_edge(ref, (NEAR * near + FAR * far, near, NEAR * near_part + FAR * far_part, near_part))


def local_kernel(field_ref, potential_ref, part_ref, low_ref, high_ref):
    planes, rows, _ = part_ref.shape
    for z in range(planes):
        for start in range(0, rows, ROWS):
            part_ref[z, pl.ds(start, ROWS)] = stencil(field_ref, potential_ref, z, start, ROWS)
    edge(low_ref, field_ref[0], field_ref[1], part_ref[0], part_ref[1])
    edge(high_ref, field_ref[3], field_ref[2], part_ref[3], part_ref[2])


def member(place, size, first):
    return (first + place) % size


def fold(product):
    folded = jnp.sum(product.reshape(-1, 8, product.shape[-1]), axis=0)
    return folded[:, :128] + folded[:, 128:]


def product_rows(rounded_ref, partners_ref, out_ref):
    count, planes, rows, _ = partners_ref.shape
    totals = [jnp.zeros((8, 128), F32)] * count
    for z in range(planes):
        for start in range(0, rows, ROWS):
            rounded = rounded_ref[z, pl.ds(start, ROWS)].astype(F32)
            for k in range(count):
                totals[k] = totals[k] + fold(rounded * partners_ref[k, z, pl.ds(start, ROWS)].astype(F32))
    for k, total in enumerate(totals):
        out_ref[pl.ds(k, 1), :] = jnp.sum(total, axis=0, keepdims=True)


def filter_kernel(
    field_ref, potential_ref, part_ref, left_ref, right_ref, partners_ref, filtered_hbm, rounded_ref, rows_ref, first_ref, filtered_ref, sems
):
    planes, rows, _ = part_ref.shape
    sides = (left_ref, load_scales(left_ref), 0, 1), (right_ref, load_scales(right_ref), 3, 2)
    for ref, scales, near, far in sides:
        for start in range(0, rows, ROWS):
            block = pl.ds(start, ROWS)
            first_ref[near, block] = part_ref[near, block] + load_edge(ref, scales, 0, start, ROWS)
            first_ref[far, block] = part_ref[far, block] + FAR * load_edge(ref, scales, 1, start, ROWS)
    totals = [jnp.zeros((8, 128), F32)] * partners_ref.shape[0]
    copies = []
    for ref, scales, nearest, second in sides:
        for z in (nearest, second):
            for start in range(0, rows, ROWS):
                block = pl.ds(start, ROWS)
                value = stencil(first_ref, potential_ref, z, start, ROWS)
                f0, f1 = field_ref[nearest, block], field_ref[second, block]
                if z == nearest:
                    value = value + (load_edge(ref, scales, 2, start, ROWS) + ((NEAR * NEAR + FAR * FAR) * f0 + (NEAR * FAR) * f1))
                else:
                    value = value + FAR * (load_edge(ref, scales, 3, start, ROWS) + (NEAR * f0 + FAR * f1))
                filtered = 2.0 * value - (f0 if z == nearest else f1)
                filtered_ref[z, block] = filtered
                rounded = filtered.astype(BF16)
                rounded_ref[z, block] = rounded
                rounded = rounded.astype(F32)
                for k in range(len(totals)):
                    totals[k] = totals[k] + fold(rounded * partners_ref[k, z, block].astype(F32))
            copy = pltpu.make_async_copy(filtered_ref.at[z], filtered_hbm.at[z], sems.at[z])
            copy.start()
            copies.append(copy)
    for k, total in enumerate(totals):
        rows_ref[pl.ds(k, 1), :] = jnp.sum(total, axis=0, keepdims=True)
    for copy in copies:
        copy.wait()


def products_kernel(rounded_ref, partners_ref, own_ref, out_ref, other_ref):
    product_rows(rounded_ref, partners_ref, other_ref)
    core = lax.axis_index("core")
    own, other = own_ref[...], other_ref[...]
    rows = jnp.where(core == 0, own, other), jnp.where(core == 0, other, own)
    for place in range(out_ref.shape[0]):
        device = member(place, out_ref.shape[0], LAYER_FIRST)
        y = (device // 2 - Y_FIRST) % 4
        out_ref[pl.ds(place, 1), :] = rows[device % 2][y : y + 1]


def owners_kernel(places_ref, parts_ref, out_ref):
    totals = [jnp.zeros((1, 128), F32)] * ORBS
    for place in range(parts_ref.shape[0]):
        owner = member(place, parts_ref.shape[0], LAYER_FIRST) % ORBS
        totals[owner] = totals[owner] + parts_ref[pl.ds(place, 1), :]
    places = places_ref[...]
    chosen = jnp.zeros(places.shape, F32)
    for owner in range(ORBS):
        chosen = jnp.where(places == owner, totals[owner], chosen)
    sums = jnp.sum(chosen, axis=1, keepdims=True)
    row = lax.broadcasted_iota(jnp.int32, chosen.shape, 0)
    lane = lax.broadcasted_iota(jnp.int32, chosen.shape, 1)
    line = jnp.sum(jnp.where(row == lane, sums, 0.0), axis=0, keepdims=True)
    out_ref[...] = jnp.broadcast_to(line, out_ref.shape)


def last_kernel(parts_ref, out_ref):
    out_ref[...] = jnp.sum(parts_ref[...], axis=0, keepdims=True)[:, :STEPS] * FACTOR


def call(kernel, shapes, args, spaces=None, scratch=(), cost=None, out_spaces=None):
    spaces = spaces or [VMEM] * len(args)
    return pl.pallas_call(
        kernel,
        out_shape=shapes,
        in_specs=[pl.BlockSpec(memory_space=space) for space in spaces],
        out_specs=[pl.BlockSpec(memory_space=space) for space in out_spaces or [VMEM] * len(shapes)],
        scratch_shapes=list(scratch),
        compiler_params=pltpu.CompilerParams(vmem_limit_bytes=8 * 1024 * 1024),
        cost_estimate=cost,
    )(*args)


def from_middle(size, first):
    return [[(first + i) % size for i in range(size)]]


def shards(orbitals, potential, partners, owners):
    grid = ("z", "x")
    count = lax.axis_size(grid)
    up = [(i, (i + 1) % count) for i in range(count)]
    down = [(i, (i - 1) % count) for i in range(count)]
    _, planes, rows, columns = orbitals.shape
    shape = jax.ShapeDtypeStruct
    slab, edges = shape((planes, rows, columns), F32), shape((4 * rows + 16, columns), jnp.int16)

    copies = jnp.broadcast_to(partners, (4,) + partners.shape[1:])
    copies, orbitals = lax.optimization_barrier((copies, orbitals))
    partners = lax.all_to_all(copies, "y", 0, 0, tiled=True, axis_index_groups=from_middle(4, Y_FIRST))
    part, low, high = call(local_kernel, (slab, edges, edges), (orbitals[0], potential))
    left = lax.ppermute(high, grid, up)
    right = lax.ppermute(low, grid, down)
    owners, right = lax.optimization_barrier((owners, right))
    places = jnp.broadcast_to(jnp.pad(owners, (0, ORBS - STEPS), constant_values=ORBS)[:, None], (ORBS, 128))
    partners, left = lax.optimization_barrier((partners, left))
    others = lax.ppermute(partners, "core", [(0, 1), (1, 0)])
    filtered, rounded, own = call(
        filter_kernel,
        (slab, shape(slab.shape, BF16), shape((4, 128), F32)),
        (orbitals[0], potential, part, left, right, partners),
        scratch=(pltpu.VMEM(slab.shape, F32), pltpu.VMEM(slab.shape, F32), pltpu.SemaphoreType.DMA((planes,))),
        cost=pl.CostEstimate(flops=10**10, bytes_accessed=10**6, transcendentals=0),
        out_spaces=(pl.ANY, VMEM, VMEM),
    )
    rounded, places = lax.optimization_barrier((rounded, places))
    parts = call(products_kernel, (shape((4 * ORBS, 128), F32),), (rounded, others, own), scratch=(pltpu.VMEM((4, 128), F32),))[0]
    layer = ("x", "y", "core")
    parts = lax.all_to_all(parts, layer, 0, 0, tiled=True, axis_index_groups=from_middle(4 * ORBS, LAYER_FIRST))
    depth = lax.axis_size("z")
    parts = call(owners_kernel, (shape((depth, 128), F32),), (places, parts))[0]
    parts = lax.all_to_all(parts, "z", 0, 0, tiled=True, axis_index_groups=from_middle(depth, Z_FIRST))
    intersection = call(last_kernel, (shape((1, STEPS), F32),), (parts,))[0]
    return filtered[None], intersection.T


def solution(mesh):
    fine = Mesh(mesh.devices.reshape(16, 4, 4, 2), ("z", "x", "y", "core"))
    grid, band = ("z", "x"), ("y", "core")
    in_specs = (P(band, grid, None, None), P(grid, None, None), P(band, grid, None, None), P())
    out_specs = (P(band, grid, None, None), P(None, band))
    return jax.shard_map(shards, mesh=fine, in_specs=in_specs, out_specs=out_specs, check_vma=False)
```

```python
import jax
import jax.numpy as jnp
from jax import lax
from jax.experimental import pallas as pl
from jax.experimental.pallas import tpu as pltpu
from jax.sharding import Mesh, PartitionSpec as P

STEPS = 6
ORBS = 8
CELLS = 256 * 128 * 256
FACTOR = float(CELLS) ** -0.5

DIAGONAL = 3.75 - 5.0
NEAR = -0.5 * (4.0 / 3.0) / 4.0
FAR = -0.5 * (-1.0 / 12.0) / 4.0

VMEM = pltpu.VMEM
SMEM = pltpu.SMEM
F32 = jnp.float32
BF16 = jnp.bfloat16

ROWS = 32

Z_FIRST = 8
LAYER_FIRST = 21
Y_FIRST = 0


def lateral(ref, z, start, count):
    rows, columns = ref.shape[1:]
    if start == 0:
        wide = jnp.concatenate([ref[z, rows - 8 : rows], ref[z, 0 : count + 8]], axis=0)
    elif start + count == rows:
        wide = jnp.concatenate([ref[z, start - 8 : rows], ref[z, 0:8]], axis=0)
    else:
        wide = ref[z, start - 8 : start + count + 8]
    center = wide[8 : 8 + count]
    near = pltpu.roll(center, 1, 1) + pltpu.roll(center, columns - 1, 1)
    far = pltpu.roll(center, 2, 1) + pltpu.roll(center, columns - 2, 1)
    near = near + (pltpu.roll(wide, 1, 0)[8 : 8 + count] + pltpu.roll(wide, count + 15, 0)[8 : 8 + count])
    far = far + (pltpu.roll(wide, 2, 0)[8 : 8 + count] + pltpu.roll(wide, count + 14, 0)[8 : 8 + count])
    return center, near, far


def stencil(ref, potential_ref, z, start, count):
    block = pl.ds(start, count)
    center, near, far = lateral(ref, z, start, count)
    for other in (z - 1, z + 1):
        if 0 <= other < ref.shape[0]:
            near = near + ref[other, block]
    for other in (z - 2, z + 2):
        if 0 <= other < ref.shape[0]:
            far = far + ref[other, block]
    return (0.25 * (potential_ref[z, block] + DIAGONAL)) * center + (NEAR * near + FAR * far)


def spread_kernel(source_ref, out_ref, sems):
    copies = [pltpu.make_async_copy(source_ref, out_ref.at[k], sems.at[k]) for k in range(out_ref.shape[0])]
    for copy in copies:
        copy.start()
    for copy in copies:
        copy.wait()


def store_edge(ref, planes):
    rows = planes[0].shape[0]
    place = lax.broadcasted_iota(jnp.int32, (16, planes[0].shape[1]), 0)
    exponents = jnp.zeros(place.shape, jnp.int32)
    for k, plane in enumerate(planes):
        largest = jnp.maximum(jnp.max(jnp.abs(plane), axis=0, keepdims=True), 1e-30)
        exponent = jnp.floor(jnp.log2(largest)) + 2.0
        ref[pl.ds(k * rows, rows), :] = jnp.round(plane * jnp.exp2(15.0 - exponent)).astype(jnp.int32).astype(jnp.int16)
        exponents = jnp.where(place == k, exponent.astype(jnp.int32), exponents)
    ref[pl.ds(len(planes) * rows, 16), :] = exponents.astype(jnp.int16)


def load_scales(ref):
    exponents = ref[pl.ds(ref.shape[0] - 16, 16), :].astype(jnp.int32).astype(F32)
    return jnp.exp2(exponents - 15.0)


def load_edge(ref, scales, k, start, count):
    rows = (ref.shape[0] - 16) // 4
    return ref[pl.ds(k * rows + start, count), :].astype(jnp.int32).astype(F32) * scales[k : k + 1]


def edge(ref, near, far, near_part, far_part):
    store_edge(ref, (NEAR * near + FAR * far, near, NEAR * near_part + FAR * far_part, near_part))


def local_kernel(field_ref, potential_ref, part_ref, low_ref, high_ref):
    planes, rows, _ = part_ref.shape
    for z in range(planes):
        for start in range(0, rows, ROWS):
            part_ref[z, pl.ds(start, ROWS)] = stencil(field_ref, potential_ref, z, start, ROWS)
    edge(low_ref, field_ref[0], field_ref[1], part_ref[0], part_ref[1])
    edge(high_ref, field_ref[3], field_ref[2], part_ref[3], part_ref[2])


def member(place, size, first):
    return (first + place) % size


def fold(product):
    folded = jnp.sum(product.reshape(-1, 8, product.shape[-1]), axis=0)
    return folded[:, :128] + folded[:, 128:]


def product_rows(rounded_ref, partners_ref, out_ref):
    count, planes, rows, _ = partners_ref.shape
    totals = [jnp.zeros((8, 128), F32)] * count
    for z in range(planes):
        for start in range(0, rows, ROWS):
            rounded = rounded_ref[z, pl.ds(start, ROWS)].astype(F32)
            for k in range(count):
                totals[k] = totals[k] + fold(rounded * partners_ref[k, z, pl.ds(start, ROWS)].astype(F32))
    for k, total in enumerate(totals):
        out_ref[pl.ds(k, 1), :] = jnp.sum(total, axis=0, keepdims=True)


def filter_kernel(
    field_ref, potential_ref, part_ref, left_ref, right_ref, partners_ref, filtered_hbm, rounded_ref, rows_ref, first_ref, filtered_ref, sems
):
    planes, rows, _ = part_ref.shape
    sides = (left_ref, load_scales(left_ref), 0, 1), (right_ref, load_scales(right_ref), 3, 2)
    for ref, scales, near, far in sides:
        for start in range(0, rows, ROWS):
            block = pl.ds(start, ROWS)
            first_ref[near, block] = part_ref[near, block] + load_edge(ref, scales, 0, start, ROWS)
            first_ref[far, block] = part_ref[far, block] + FAR * load_edge(ref, scales, 1, start, ROWS)
    totals = [jnp.zeros((8, 128), F32)] * partners_ref.shape[0]
    copies = []
    for ref, scales, nearest, second in sides:
        for z in (nearest, second):
            for start in range(0, rows, ROWS):
                block = pl.ds(start, ROWS)
                value = stencil(first_ref, potential_ref, z, start, ROWS)
                f0, f1 = field_ref[nearest, block], field_ref[second, block]
                if z == nearest:
                    value = value + (load_edge(ref, scales, 2, start, ROWS) + ((NEAR * NEAR + FAR * FAR) * f0 + (NEAR * FAR) * f1))
                else:
                    value = value + FAR * (load_edge(ref, scales, 3, start, ROWS) + (NEAR * f0 + FAR * f1))
                filtered = 2.0 * value - (f0 if z == nearest else f1)
                filtered_ref[z, block] = filtered
                rounded = filtered.astype(BF16)
                rounded_ref[z, block] = rounded
                rounded = rounded.astype(F32)
                for k in range(len(totals)):
                    totals[k] = totals[k] + fold(rounded * partners_ref[k, z, block].astype(F32))
            copy = pltpu.make_async_copy(filtered_ref.at[z], filtered_hbm.at[z], sems.at[z])
            copy.start()
            copies.append(copy)
    for k, total in enumerate(totals):
        rows_ref[pl.ds(k, 1), :] = jnp.sum(total, axis=0, keepdims=True)
    for copy in copies:
        copy.wait()


def products_kernel(rounded_ref, partners_ref, own_ref, out_ref, other_ref):
    product_rows(rounded_ref, partners_ref, other_ref)
    core = lax.axis_index("core")
    own, other = own_ref[...], other_ref[...]
    rows = jnp.where(core == 0, own, other), jnp.where(core == 0, other, own)
    for place in range(out_ref.shape[0]):
        device = member(place, out_ref.shape[0], LAYER_FIRST)
        y = (device // 2 - Y_FIRST) % 4
        out_ref[pl.ds(place, 1), :] = rows[device % 2][y : y + 1]


def owners_kernel(places_ref, parts_ref, out_ref):
    totals = [jnp.zeros((1, 128), F32)] * ORBS
    for place in range(parts_ref.shape[0]):
        owner = member(place, parts_ref.shape[0], LAYER_FIRST) % ORBS
        totals[owner] = totals[owner] + parts_ref[pl.ds(place, 1), :]
    places = places_ref[...]
    chosen = jnp.zeros(places.shape, F32)
    for owner in range(ORBS):
        chosen = jnp.where(places == owner, totals[owner], chosen)
    sums = jnp.sum(chosen, axis=1, keepdims=True)
    row = lax.broadcasted_iota(jnp.int32, chosen.shape, 0)
    lane = lax.broadcasted_iota(jnp.int32, chosen.shape, 1)
    line = jnp.sum(jnp.where(row == lane, sums, 0.0), axis=0, keepdims=True)
    out_ref[...] = jnp.broadcast_to(line, out_ref.shape)


def last_kernel(parts_ref, out_ref):
    out_ref[...] = jnp.sum(parts_ref[...], axis=0, keepdims=True)[:, :STEPS] * FACTOR


def call(kernel, shapes, args, spaces=None, scratch=(), cost=None, out_spaces=None):
    spaces = spaces or [VMEM] * len(args)
    return pl.pallas_call(
        kernel,
        out_shape=shapes,
        in_specs=[pl.BlockSpec(memory_space=space) for space in spaces],
        out_specs=[pl.BlockSpec(memory_space=space) for space in out_spaces or [VMEM] * len(shapes)],
        scratch_shapes=list(scratch),
        compiler_params=pltpu.CompilerParams(vmem_limit_bytes=8 * 1024 * 1024),
        cost_estimate=cost,
    )(*args)


def from_middle(size, first):
    return [[(first + i) % size for i in range(size)]]


def shards(orbitals, potential, partners, owners):
    grid = ("z", "x")
    count = lax.axis_size(grid)
    up = [(i, (i + 1) % count) for i in range(count)]
    down = [(i, (i - 1) % count) for i in range(count)]
    _, planes, rows, columns = orbitals.shape
    shape = jax.ShapeDtypeStruct
    slab, edges = shape((planes, rows, columns), F32), shape((4 * rows + 16, columns), jnp.int16)

    copies = call(
        spread_kernel,
        (shape((4, planes, rows, columns), BF16),),
        (partners[0],),
        scratch=(pltpu.SemaphoreType.DMA((4,)),),
        out_spaces=(pl.ANY,),
    )[0]
    partners = lax.all_to_all(copies, "y", 0, 0, tiled=True, axis_index_groups=from_middle(4, Y_FIRST))
    part, low, high = call(local_kernel, (slab, edges, edges), (orbitals[0], potential))
    left = lax.ppermute(high, grid, up)
    right = lax.ppermute(low, grid, down)
    owners, right = lax.optimization_barrier((owners, right))
    places = jnp.broadcast_to(jnp.pad(owners, (0, ORBS - STEPS), constant_values=ORBS)[:, None], (ORBS, 128))
    partners, left = lax.optimization_barrier((partners, left))
    others = lax.ppermute(partners, "core", [(0, 1), (1, 0)])
    filtered, rounded, own = call(
        filter_kernel,
        (slab, shape(slab.shape, BF16), shape((4, 128), F32)),
        (orbitals[0], potential, part, left, right, partners),
        scratch=(pltpu.VMEM(slab.shape, F32), pltpu.VMEM(slab.shape, F32), pltpu.SemaphoreType.DMA((planes,))),
        cost=pl.CostEstimate(flops=10**10, bytes_accessed=10**6, transcendentals=0),
        out_spaces=(pl.ANY, VMEM, VMEM),
    )
    rounded, places = lax.optimization_barrier((rounded, places))
    parts = call(products_kernel, (shape((4 * ORBS, 128), F32),), (rounded, others, own), scratch=(pltpu.VMEM((4, 128), F32),))[0]
    layer = ("x", "y", "core")
    parts = lax.all_to_all(parts, layer, 0, 0, tiled=True, axis_index_groups=from_middle(4 * ORBS, LAYER_FIRST))
    depth = lax.axis_size("z")
    parts = call(owners_kernel, (shape((depth, 128), F32),), (places, parts))[0]
    parts = lax.all_to_all(parts, "z", 0, 0, tiled=True, axis_index_groups=from_middle(depth, Z_FIRST))
    intersection = call(last_kernel, (shape((1, STEPS), F32),), (parts,))[0]
    return filtered[None], intersection.T


def solution(mesh):
    fine = Mesh(mesh.devices.reshape(16, 4, 4, 2), ("z", "x", "y", "core"))
    grid, band = ("z", "x"), ("y", "core")
    in_specs = (P(band, grid, None, None), P(grid, None, None), P(band, grid, None, None), P())
    out_specs = (P(band, grid, None, None), P(None, band))
    return jax.shard_map(shards, mesh=fine, in_specs=in_specs, out_specs=out_specs, check_vma=False)
```

```python
import jax
import jax.numpy as jnp
from jax import lax
from jax.experimental import pallas as pl
from jax.experimental.pallas import tpu as pltpu
from jax.sharding import Mesh, PartitionSpec as P

STEPS = 6
ORBS = 8
CELLS = 256 * 128 * 256
FACTOR = float(CELLS) ** -0.5

DIAGONAL = 3.75 - 5.0
NEAR = -0.5 * (4.0 / 3.0) / 4.0
FAR = -0.5 * (-1.0 / 12.0) / 4.0

VMEM = pltpu.VMEM
SMEM = pltpu.SMEM
F32 = jnp.float32
BF16 = jnp.bfloat16

ROWS = 64

Z_FIRST = 8
LAYER_FIRST = 21
Y_FIRST = 0


def lateral(ref, z, start, count):
    rows, columns = ref.shape[1:]
    if start == 0:
        wide = jnp.concatenate([ref[z, rows - 8 : rows], ref[z, 0 : count + 8]], axis=0)
    elif start + count == rows:
        wide = jnp.concatenate([ref[z, start - 8 : rows], ref[z, 0:8]], axis=0)
    else:
        wide = ref[z, start - 8 : start + count + 8]
    center = wide[8 : 8 + count]
    near = pltpu.roll(center, 1, 1) + pltpu.roll(center, columns - 1, 1)
    far = pltpu.roll(center, 2, 1) + pltpu.roll(center, columns - 2, 1)
    near = near + (pltpu.roll(wide, 1, 0)[8 : 8 + count] + pltpu.roll(wide, count + 15, 0)[8 : 8 + count])
    far = far + (pltpu.roll(wide, 2, 0)[8 : 8 + count] + pltpu.roll(wide, count + 14, 0)[8 : 8 + count])
    return center, near, far


def stencil(ref, potential_ref, z, start, count):
    block = pl.ds(start, count)
    center, near, far = lateral(ref, z, start, count)
    for other in (z - 1, z + 1):
        if 0 <= other < ref.shape[0]:
            near = near + ref[other, block]
    for other in (z - 2, z + 2):
        if 0 <= other < ref.shape[0]:
            far = far + ref[other, block]
    return (0.25 * (potential_ref[z, block] + DIAGONAL)) * center + (NEAR * near + FAR * far)


def spread_kernel(source_ref, out_ref, sems):
    copies = [pltpu.make_async_copy(source_ref, out_ref.at[k], sems.at[k]) for k in range(out_ref.shape[0])]
    for copy in copies:
        copy.start()
    for copy in copies:
        copy.wait()


def store_edge(ref, planes):
    rows = planes[0].shape[0]
    place = lax.broadcasted_iota(jnp.int32, (16, planes[0].shape[1]), 0)
    exponents = jnp.zeros(place.shape, jnp.int32)
    for k, plane in enumerate(planes):
        largest = jnp.maximum(jnp.max(jnp.abs(plane), axis=0, keepdims=True), 1e-30)
        exponent = jnp.floor(jnp.log2(largest)) + 2.0
        ref[pl.ds(k * rows, rows), :] = jnp.round(plane * jnp.exp2(15.0 - exponent)).astype(jnp.int32).astype(jnp.int16)
        exponents = jnp.where(place == k, exponent.astype(jnp.int32), exponents)
    ref[pl.ds(len(planes) * rows, 16), :] = exponents.astype(jnp.int16)


def load_scales(ref):
    exponents = ref[pl.ds(ref.shape[0] - 16, 16), :].astype(jnp.int32).astype(F32)
    return jnp.exp2(exponents - 15.0)


def load_edge(ref, scales, k, start, count):
    rows = (ref.shape[0] - 16) // 4
    return ref[pl.ds(k * rows + start, count), :].astype(jnp.int32).astype(F32) * scales[k : k + 1]


def edge(ref, near, far, near_part, far_part):
    store_edge(ref, (NEAR * near + FAR * far, near, NEAR * near_part + FAR * far_part, near_part))


def local_kernel(field_ref, potential_ref, part_ref, low_ref, high_ref):
    planes, rows, _ = part_ref.shape
    for z in range(planes):
        for start in range(0, rows, ROWS):
            part_ref[z, pl.ds(start, ROWS)] = stencil(field_ref, potential_ref, z, start, ROWS)
    edge(low_ref, field_ref[0], field_ref[1], part_ref[0], part_ref[1])
    edge(high_ref, field_ref[3], field_ref[2], part_ref[3], part_ref[2])


def member(place, size, first):
    return (first + place) % size


def fold(product):
    folded = jnp.sum(product.reshape(-1, 8, product.shape[-1]), axis=0)
    return folded[:, :128] + folded[:, 128:]


def product_rows(rounded_ref, partners_ref, out_ref):
    count, planes, rows, _ = partners_ref.shape
    totals = [jnp.zeros((8, 128), F32)] * count
    for z in range(planes):
        for start in range(0, rows, ROWS):
            rounded = rounded_ref[z, pl.ds(start, ROWS)].astype(F32)
            for k in range(count):
                totals[k] = totals[k] + fold(rounded * partners_ref[k, z, pl.ds(start, ROWS)].astype(F32))
    for k, total in enumerate(totals):
        out_ref[pl.ds(k, 1), :] = jnp.sum(total, axis=0, keepdims=True)


def filter_kernel(
    field_ref, potential_ref, part_ref, left_ref, right_ref, partners_ref, filtered_hbm, rounded_ref, rows_ref, first_ref, filtered_ref, sems
):
    planes, rows, _ = part_ref.shape
    sides = (left_ref, load_scales(left_ref), 0, 1), (right_ref, load_scales(right_ref), 3, 2)
    for ref, scales, near, far in sides:
        for start in range(0, rows, ROWS):
            block = pl.ds(start, ROWS)
            first_ref[near, block] = part_ref[near, block] + load_edge(ref, scales, 0, start, ROWS)
            first_ref[far, block] = part_ref[far, block] + FAR * load_edge(ref, scales, 1, start, ROWS)
    totals = [jnp.zeros((8, 128), F32)] * partners_ref.shape[0]
    copies = []
    for ref, scales, nearest, second in sides:
        for z in (nearest, second):
            for start in range(0, rows, ROWS):
                block = pl.ds(start, ROWS)
                value = stencil(first_ref, potential_ref, z, start, ROWS)
                f0, f1 = field_ref[nearest, block], field_ref[second, block]
                if z == nearest:
                    value = value + (load_edge(ref, scales, 2, start, ROWS) + ((NEAR * NEAR + FAR * FAR) * f0 + (NEAR * FAR) * f1))
                else:
                    value = value + FAR * (load_edge(ref, scales, 3, start, ROWS) + (NEAR * f0 + FAR * f1))
                filtered = 2.0 * value - (f0 if z == nearest else f1)
                filtered_ref[z, block] = filtered
                rounded = filtered.astype(BF16)
                rounded_ref[z, block] = rounded
                rounded = rounded.astype(F32)
                for k in range(len(totals)):
                    totals[k] = totals[k] + fold(rounded * partners_ref[k, z, block].astype(F32))
            copy = pltpu.make_async_copy(filtered_ref.at[z], filtered_hbm.at[z], sems.at[z])
            copy.start()
            copies.append(copy)
    for k, total in enumerate(totals):
        rows_ref[pl.ds(k, 1), :] = jnp.sum(total, axis=0, keepdims=True)
    for copy in copies:
        copy.wait()


def products_kernel(rounded_ref, partners_ref, own_ref, out_ref, other_ref):
    product_rows(rounded_ref, partners_ref, other_ref)
    core = lax.axis_index("core")
    own, other = own_ref[...], other_ref[...]
    rows = jnp.where(core == 0, own, other), jnp.where(core == 0, other, own)
    for place in range(out_ref.shape[0]):
        device = member(place, out_ref.shape[0], LAYER_FIRST)
        y = (device // 2 - Y_FIRST) % 4
        out_ref[pl.ds(place, 1), :] = rows[device % 2][y : y + 1]


def owners_kernel(places_ref, parts_ref, out_ref):
    totals = [jnp.zeros((1, 128), F32)] * ORBS
    for place in range(parts_ref.shape[0]):
        owner = member(place, parts_ref.shape[0], LAYER_FIRST) % ORBS
        totals[owner] = totals[owner] + parts_ref[pl.ds(place, 1), :]
    places = places_ref[...]
    chosen = jnp.zeros(places.shape, F32)
    for owner in range(ORBS):
        chosen = jnp.where(places == owner, totals[owner], chosen)
    sums = jnp.sum(chosen, axis=1, keepdims=True)
    row = lax.broadcasted_iota(jnp.int32, chosen.shape, 0)
    lane = lax.broadcasted_iota(jnp.int32, chosen.shape, 1)
    line = jnp.sum(jnp.where(row == lane, sums, 0.0), axis=0, keepdims=True)
    out_ref[...] = jnp.broadcast_to(line, out_ref.shape)


def last_kernel(parts_ref, out_ref):
    out_ref[...] = jnp.sum(parts_ref[...], axis=0, keepdims=True)[:, :STEPS] * FACTOR


def call(kernel, shapes, args, spaces=None, scratch=(), cost=None, out_spaces=None):
    spaces = spaces or [VMEM] * len(args)
    return pl.pallas_call(
        kernel,
        out_shape=shapes,
        in_specs=[pl.BlockSpec(memory_space=space) for space in spaces],
        out_specs=[pl.BlockSpec(memory_space=space) for space in out_spaces or [VMEM] * len(shapes)],
        scratch_shapes=list(scratch),
        compiler_params=pltpu.CompilerParams(vmem_limit_bytes=8 * 1024 * 1024),
        cost_estimate=cost,
    )(*args)


def from_middle(size, first):
    return [[(first + i) % size for i in range(size)]]


def shards(orbitals, potential, partners, owners):
    grid = ("z", "x")
    count = lax.axis_size(grid)
    up = [(i, (i + 1) % count) for i in range(count)]
    down = [(i, (i - 1) % count) for i in range(count)]
    _, planes, rows, columns = orbitals.shape
    shape = jax.ShapeDtypeStruct
    slab, edges = shape((planes, rows, columns), F32), shape((4 * rows + 16, columns), jnp.int16)

    copies = call(
        spread_kernel,
        (shape((4, planes, rows, columns), BF16),),
        (partners[0],),
        scratch=(pltpu.SemaphoreType.DMA((4,)),),
        out_spaces=(pl.ANY,),
    )[0]
    partners = lax.all_to_all(copies, "y", 0, 0, tiled=True, axis_index_groups=from_middle(4, Y_FIRST))
    part, low, high = call(local_kernel, (slab, edges, edges), (orbitals[0], potential))
    left = lax.ppermute(high, grid, up)
    right = lax.ppermute(low, grid, down)
    owners, right = lax.optimization_barrier((owners, right))
    places = jnp.broadcast_to(jnp.pad(owners, (0, ORBS - STEPS), constant_values=ORBS)[:, None], (ORBS, 128))
    partners, left = lax.optimization_barrier((partners, left))
    others = lax.ppermute(partners, "core", [(0, 1), (1, 0)])
    filtered, rounded, own = call(
        filter_kernel,
        (slab, shape(slab.shape, BF16), shape((4, 128), F32)),
        (orbitals[0], potential, part, left, right, partners),
        scratch=(pltpu.VMEM(slab.shape, F32), pltpu.VMEM(slab.shape, F32), pltpu.SemaphoreType.DMA((planes,))),
        cost=pl.CostEstimate(flops=10**10, bytes_accessed=10**6, transcendentals=0),
        out_spaces=(pl.ANY, VMEM, VMEM),
    )
    rounded, places = lax.optimization_barrier((rounded, places))
    parts = call(products_kernel, (shape((4 * ORBS, 128), F32),), (rounded, others, own), scratch=(pltpu.VMEM((4, 128), F32),))[0]
    layer = ("x", "y", "core")
    parts = lax.all_to_all(parts, layer, 0, 0, tiled=True, axis_index_groups=from_middle(4 * ORBS, LAYER_FIRST))
    depth = lax.axis_size("z")
    parts = call(owners_kernel, (shape((depth, 128), F32),), (places, parts))[0]
    parts = lax.all_to_all(parts, "z", 0, 0, tiled=True, axis_index_groups=from_middle(depth, Z_FIRST))
    intersection = call(last_kernel, (shape((1, STEPS), F32),), (parts,))[0]
    return filtered[None], intersection.T


def solution(mesh):
    fine = Mesh(mesh.devices.reshape(16, 4, 4, 2), ("z", "x", "y", "core"))
    grid, band = ("z", "x"), ("y", "core")
    in_specs = (P(band, grid, None, None), P(grid, None, None), P(band, grid, None, None), P())
    out_specs = (P(band, grid, None, None), P(None, band))
    return jax.shard_map(shards, mesh=fine, in_specs=in_specs, out_specs=out_specs, check_vma=False)
```
